32 devices in a mesh: proto: 16 (over z, y, core), rows: 2 (over x).
Axes of the slice: x: 2, y: 2, z: 4, core: 2. Of those that a mesh axis runs over, the one named last changes fastest.
Arguments:
- student: float32 [2048, 384], P('rows'), may hold values from -15 to 15
- teacher: float32 [2048, 384], P('rows'), may hold values from -30 to 30
- proto_raw: float32 [384, 8192], P(None, 'proto'), may hold values from -60 to 60
- weights: float32 [2048], P('rows'), may hold values from 0.25 to 4
- mask: int32 [2048], P('rows'), may hold values from 0 to 1, as said below
Outputs:
- grad_student: float32 [2048, 384], P('rows')
- grad_proto: float32 [384, 8192], P('rows', 'proto')
The draws below stay inside these ranges and needn't reach their ends.
Inputs may be any that keep to these rules, and one draw needn't show every extreme that they name: `mask`: row 0 is always 1.
All inputs are finite; a program needn't handle non-finite values.
Results may differ from the reference program's by a relative error of at most 0.00029.
Values sent between devices are 32-bit elements; how exact they have to be, the bound alone decides.
A program may use at most 64 MiB of HBM per device.

```python
import math
import jax
import jax.numpy as jnp
from jax import lax

D = 384
P_DEV = 512
ITERS = 3
PROTO = 8192
ROWS = 2048


hot_count = 256


def columns_all(key):
    return jnp.clip(jax.random.normal(jax.random.fold_in(key, 101), (D, PROTO), jnp.float32), -6.0, 6.0)


def chosen_columns(key):
    hot_pool = jax.random.randint(jax.random.fold_in(key, 102), (hot_count,), 0, PROTO)
    picked = jax.random.randint(jax.random.fold_in(key, 103), (ROWS,), 0, hot_count)
    return hot_pool[picked]


def drawn_rows(key, salt_value, low_end, high_end):
    anchors = jnp.take(columns_all(key), chosen_columns(key), axis=1).T
    strength = jnp.exp(jax.random.uniform(jax.random.fold_in(key, salt_value), (ROWS, 1), jnp.float32, math.log(low_end), math.log(high_end)))
    noise_key = jax.random.fold_in(key, salt_value + 1)
    jitter = jnp.clip(jax.random.normal(noise_key, (ROWS, D), jnp.float32), -6.0, 6.0)
    return strength * anchors + jitter


def draw_teacher(key, part):
    return drawn_rows(key, 201, 0.5, 3.0)


def draw_student(key, part):
    return drawn_rows(key, 301, 0.25, 1.0)


def draw_proto_raw(key, part):
    columns = columns_all(key)
    return columns


def draw_mask(key, part):
    coins = jax.random.randint(jax.random.fold_in(key, 104), (ROWS,), 0, 4)
    chosen = jnp.where(coins < 3, 1, 0).astype(jnp.int32)
    leading = jnp.arange(ROWS) == 0
    return jnp.where(leading, 1, chosen).astype(jnp.int32)


def levels(stream_key, dims, cuts, smallest, top_value):
    gain, own = 1.0, jax.random.fold_in(stream_key, 6)
    for dim, shards_of in cuts:
        steps = jnp.exp(jax.random.uniform(jax.random.fold_in(own, dim), (shards_of,), jnp.float32, smallest / len(cuts), top_value / len(cuts)))
        gain = gain * jnp.repeat(steps, dims[dim] // shards_of).reshape([-1 if axis == dim else 1 for axis in range(len(dims))])
    return gain


def setup_inputs(seed: int = 0) -> dict:
    streams_of = jax.random.split(jax.random.key(seed), 6)
    student = draw_student(jax.random.fold_in(streams_of[5], 71), 0)
    teacher = draw_teacher(jax.random.fold_in(streams_of[5], 71), 0)
    proto_raw = draw_proto_raw(jax.random.fold_in(streams_of[5], 71), 0)
    weights = jnp.clip(jnp.exp(math.log(4.0) - 2.7725887 * jax.random.uniform(streams_of[3], (ROWS,), jnp.float32) ** levels(streams_of[3], (ROWS,), ((0, 2),), -0.2, 0.2)), 0.25, 4.0)
    mask = draw_mask(jax.random.fold_in(streams_of[5], 71), 0)
    return {"student": student, "teacher": teacher, "proto_raw": proto_raw, "weights": weights, "mask": mask}


eps = 1e-06
teach_temp = 0.07
student_temp = 0.1

def unit_rows(values):
    scale = lax.rsqrt(lax.optimization_barrier(jnp.sum(values * values, axis=1, keepdims=True)) + eps)
    return (values * scale, scale)

def unit_cols(values):
    scale = lax.rsqrt(lax.optimization_barrier(jnp.sum(values * values, axis=0, keepdims=True)) + eps)
    return (values * scale, scale)

def reference(student, teacher, proto_raw, weights, mask):
    highest = lax.Precision.HIGHEST
    s_n, s_scale = unit_rows(student)
    t_n, unused = unit_rows(teacher)
    nblocks = PROTO // P_DEV
    blocks = proto_raw.reshape(D, nblocks, P_DEV).transpose(1, 0, 2)
    nrows = student.shape[0]
    mask_float = mask.astype(jnp.float32)

    def teach(block):
        w_n, unused_scale = unit_cols(block)
        return jnp.exp(jnp.dot(t_n, w_n, precision=highest) / teach_temp)

    def row_pass(col_fac):

        def step(total, item):
            block, factor = item
            return (total + lax.optimization_barrier(jnp.sum(teach(block) * factor[None, :], axis=1)), None)
        total, unused_out = lax.scan(step, jnp.zeros((nrows,), jnp.float32), (blocks, col_fac))
        return total

    def col_pass(row_fac):
        weighted = row_fac * mask_float
        return lax.map(lambda block: lax.optimization_barrier(jnp.sum(teach(block) * weighted[:, None], axis=0)), blocks)
    col_fac = jnp.ones((nblocks, P_DEV), jnp.float32)
    row_fac = 1.0 / row_pass(col_fac)
    for step in range(ITERS):
        col_fac = 1.0 / col_pass(row_fac)
        row_fac = 1.0 / row_pass(col_fac)

    def zstep(total, block):
        w_n, unused_scale = unit_cols(block)
        return (total + lax.optimization_barrier(jnp.sum(jnp.exp(jnp.dot(s_n, w_n, precision=highest) / student_temp), axis=1)), None)
    zsum, unused_z = lax.scan(zstep, jnp.zeros((nrows,), jnp.float32), blocks)
    coef = weights * mask_float

    def gstep(d_sn, item):
        block, factor = item
        w_n, c_scale = unit_cols(block)
        target = teach(block) * row_fac[:, None] * factor[None, :]
        prob = jnp.exp(jnp.dot(s_n, w_n, precision=highest) / student_temp) / zsum[:, None]
        dcos = coef[:, None] * (prob - target) / student_temp
        d_sn = d_sn + jnp.dot(dcos, w_n.T, precision=highest)
        d_wn = jnp.dot(s_n.T, dcos, precision=highest)
        grad = (d_wn - w_n * lax.optimization_barrier(jnp.sum(w_n * d_wn, axis=0, keepdims=True))) * c_scale
        return (d_sn, grad)
    d_sn, grads = lax.scan(gstep, jnp.zeros((nrows, D), jnp.float32), (blocks, col_fac))
    grad_student = (d_sn - s_n * lax.optimization_barrier(jnp.sum(s_n * d_sn, axis=1, keepdims=True))) * s_scale
    grad_proto = grads.transpose(1, 0, 2).reshape(D, PROTO)
    return (grad_student, grad_proto)
```

```python
import functools

import jax
import jax.numpy as jnp
from jax import lax
from jax.experimental import pallas as pl
from jax.experimental.pallas import tpu as pltpu
from jax.sharding import PartitionSpec as P

ITERS = 3
EPS = 1e-06
TEACH = 1.0 / 0.07
STUDENT = 1.0 / 0.1
TILES = 4
LANES = 128
f32 = jnp.float32
bf16 = jnp.bfloat16
MESH = pl.DeviceIdType.MESH


def make_levels(n):
    if n % 2:
        return [(n, 1)]
    rest = n // 2
    outer = 4 if rest == 8 else 8
    while rest % outer:
        outer //= 2
    mid = rest // outer
    levels = [(2, 1), (mid, 2), (outer, 2 * mid)]
    return [lv for lv in levels if lv[0] > 1]


def split(x):
    hi = x.astype(bf16)
    return hi, (x - hi.astype(f32)).astype(bf16)


def dot(a, b):
    return jnp.dot(a, b, preferred_element_type=f32)


def dot_t(a, b):
    return lax.dot_general(a, b, (((1,), (1,)), ((), ())), preferred_element_type=f32)


def kernel(n, nr, chunks, block, orders, student, teacher, proto, weights, mask, gs, gp, *scratch):
    (wn, cs, w_hi, w_lo, lhs, kt, et, s_hi, s_lo, d_hi, d_lo, c128, rs_out, rs_in, cp_out, cp_in,
     acc, dw, dw_in, cd_out, cd_in,
     rs_ss, rs_rs, cp_ss, cp_rs, dw_ss, dw_rs, cd_ss, cd_rs, red_ss, red_rs, gat_ss, gat_rs) = scratch[:33]
    red_in = scratch[33:]
    nl = len(orders[0])
    dim, protos = proto.shape
    rows = student.shape[0]
    tile = rows // TILES
    share = dim // nr
    me = lax.axis_index("proto")
    mx = lax.axis_index("rows")

    def peer(k):
        return {"proto": lax.rem(me + k, n)}

    def rpeer(k):
        return {"rows": lax.rem(mx + k, nr)}

    barrier = pltpu.get_barrier_semaphore()

    def greet(k, carry):
        pl.semaphore_signal(barrier, inc=1, device_id=peer(k), device_id_type=MESH)
        return carry

    lax.fori_loop(1, n, greet, 0)
    for k in range(1, nr):
        pl.semaphore_signal(barrier, inc=1, device_id=rpeer(k), device_id_type=MESH)

    for i in range(protos // LANES):
        cols = slice(i * LANES, (i + 1) * LANES)
        w = proto[:, cols]
        scale = lax.rsqrt(jnp.sum(w * w, axis=0, keepdims=True) + EPS)
        w = w * scale
        cs[:, cols] = scale
        wn[:, cols] = w
        hi, lo = split(w)
        w_hi[:, cols] = hi
        w_lo[:, cols] = lo
        hi, lo = split(w.T)
        lhs[cols, 0:dim] = hi
        lhs[cols, dim : 2 * dim] = hi
        lhs[cols, 2 * dim : 3 * dim] = lo

    def unit(x):
        return x * lax.rsqrt(jnp.sum(x * x, axis=1, keepdims=True) + EPS)

    def teach(i, carry):
        at = pl.ds(pl.multiple_of(i * tile, tile), tile)
        hi, lo = split(unit(teacher[at, :]))
        cos = dot_t(lhs[...], jnp.concatenate([hi, lo, hi], axis=1))
        q = jnp.exp(cos * TEACH)
        kt[:, at] = q
        rs_out[0, :, at] = jnp.sum(q, axis=0, keepdims=True)
        return carry

    def study(i, carry):
        at = pl.ds(pl.multiple_of(i * tile, tile), tile)
        hi, lo = split(unit(student[at, :]))
        s_hi[at, :] = hi
        s_lo[at, :] = lo
        cos = dot_t(lhs[...], jnp.concatenate([hi, lo, hi], axis=1))
        q = jnp.exp(cos * STUDENT)
        et[:, at] = q
        rs_out[ITERS + 1, :, at] = jnp.sum(q, axis=0, keepdims=True)
        return carry

    def row_start(rd):
        def send(k, carry):
            pltpu.make_async_remote_copy(
                rs_out.at[rd], rs_in.at[rd, k - 1], rs_ss.at[rd], rs_rs.at[rd],
                device_id=peer(k), device_id_type=MESH).start()
            return carry

        lax.fori_loop(1, n, send, 0)

    def row_total(rd):
        pltpu.make_async_copy(rs_in.at[rd], rs_in.at[rd], rs_rs.at[rd]).wait()
        return rs_out[rd] + jnp.sum(rs_in[rd], axis=0)

    def col_copy(it, k):
        return pltpu.make_async_remote_copy(
            cp_out.at[it], cp_in.at[it, k - 1], cp_ss.at[it, k - 1], cp_rs.at[it, k - 1],
            device_id=rpeer(k), device_id_type=MESH)

    lax.fori_loop(0, TILES, teach, 0)
    pl.semaphore_wait(barrier, n - 1 + nr - 1)
    row_start(0)
    lax.fori_loop(0, TILES, study, 0)
    row_start(ITERS + 1)
    mask_f = mask[...].astype(f32)
    r = 1.0 / row_total(0)
    for it in range(ITERS):
        rm = r * mask_f
        for i in range(protos // LANES):
            at = slice(i * LANES, (i + 1) * LANES)
            part = kt[at, 0:LANES] * rm[:, 0:LANES]
            for j in range(1, rows // LANES):
                lane = slice(j * LANES, (j + 1) * LANES)
                part = part + kt[at, lane] * rm[:, lane]
            cp_out[it, :, at] = jnp.sum(part.T, axis=0, keepdims=True)
        for k in range(1, nr):
            col_copy(it, k).start()
        total = cp_out[it]
        for k in range(1, nr):
            col_copy(it, k).wait_recv()
            total = total + cp_in[it, k - 1]
        c = 1.0 / total
        for i in range(protos // LANES):
            at = slice(i * LANES, (i + 1) * LANES)
            c128[at, :] = jnp.broadcast_to(c[:, at], (LANES, LANES)).T
        for j in range(rows // LANES):
            lane = slice(j * LANES, (j + 1) * LANES)
            rs_out[it + 1, :, lane] = jnp.sum(kt[:, lane] * c128[...], axis=0, keepdims=True)
        row_start(it + 1)
        r = 1.0 / row_total(it + 1)
    zsum = row_total(ITERS + 1)
    coef = weights[...] * mask_f * STUDENT
    pa = coef / zsum
    pb = coef * r

    state = [(0, block)] * chunks

    def place(g, l):
        size, stride = orders[g][l]
        return size, stride, lax.rem(me // stride, size)

    def red_copy(g, l, k):
        size, stride, mine = place(g, l)
        off, ln = state[g]
        sub = ln // size
        to = lax.rem(mine + k, size)
        return pltpu.make_async_remote_copy(
            acc.at[g, pl.ds(pl.multiple_of(off + to * sub, 8), sub)], red_in[g * nl + l].at[k - 1],
            red_ss.at[g, l, k - 1], red_rs.at[g, l, k - 1],
            device_id={"proto": me + (to - mine) * stride}, device_id_type=MESH)

    def red_start(g, l):
        for k in range(1, orders[g][l][0]):
            red_copy(g, l, k).start()

    def red_finish(g, l):
        size, stride, mine = place(g, l)
        off, ln = state[g]
        sub = ln // size
        for k in range(1, size):
            red_copy(g, l, k).wait_recv()
        off = pl.multiple_of(off + mine * sub, 8)
        at = pl.ds(off, sub)
        total = acc[g, at, :]
        for k in range(1, size):
            total = total + red_in[g * nl + l][k - 1]
        state[g] = (off, sub)
        if l < nl - 1:
            acc[g, at, :] = total
            return
        first = g * block + off
        first = pl.multiple_of(jnp.minimum(first, rows - sub), 8)
        st = student[pl.ds(first, sub), :]
        scale = lax.rsqrt(jnp.sum(st * st, axis=1, keepdims=True) + EPS)
        st = st * scale
        gs[g, at, :] = (total - st * jnp.sum(st * total, axis=1, keepdims=True)) * scale

    def gat_copy(g, l, k):
        size, stride, mine = place(g, l)
        off, ln = state[g]
        to = lax.rem(mine + k, size)
        at = pl.ds(pl.multiple_of(off, 8), ln)
        return pltpu.make_async_remote_copy(
            gs.at[g, at], gs.at[g, at], gat_ss.at[g, l, k - 1], gat_rs.at[g, l, k - 1],
            device_id={"proto": me + (to - mine) * stride}, device_id_type=MESH)

    def gat_start(g, l):
        for k in range(1, orders[g][l][0]):
            gat_copy(g, l, k).start()

    def gat_finish(g, l):
        size, stride, mine = place(g, l)
        off, ln = state[g]
        for k in range(1, size):
            gat_copy(g, l, k).wait_recv()
        for k in range(1, size):
            gat_copy(g, l, k).wait_send()
        state[g] = (off - mine * ln, ln * size)

    def stage(g, s):
        if s > 0:
            if s <= nl:
                red_finish(g, s - 1)
            else:
                gat_finish(g, 2 * nl - s)
        if s < nl:
            red_start(g, s)
        elif s < 2 * nl:
            gat_start(g, 2 * nl - 1 - s)

    def student_tile(i):
        at = slice(i * tile, (i + 1) * tile)
        cc = jnp.concatenate([c128[...]] * (tile // LANES), axis=1)
        hi, lo = split(et[:, at] * pa[:, at] - kt[:, at] * cc * pb[:, at])
        d_hi[:, at] = hi
        d_lo[:, at] = lo
        part = dot(w_hi[...], hi) + dot(w_lo[...], hi) + dot(w_hi[...], lo)
        g, first = divmod(i * tile, block)
        acc[g, first : first + tile, :] = part.T

    def dw_copy(k):
        to = lax.rem(mx + k, nr)
        at = pl.ds(pl.multiple_of(to * share, 8), share)
        return pltpu.make_async_remote_copy(
            dw.at[at], dw_in.at[k - 1], dw_ss.at[k - 1], dw_rs.at[k - 1],
            device_id={"rows": to}, device_id_type=MESH)

    def cd_copy(k):
        return pltpu.make_async_remote_copy(
            cd_out, cd_in.at[k - 1], cd_ss.at[k - 1], cd_rs.at[k - 1],
            device_id=rpeer(k), device_id_type=MESH)

    def proto_block(i):
        at = slice(i * LANES, (i + 1) * LANES)
        hi = d_hi[at, :]
        part = (dot(hi, s_hi[...]) + dot(hi, s_lo[...]) + dot(d_lo[at, :], s_hi[...])).T
        dw[:, at] = part
        cd_out[:, at] = jnp.sum(part * wn[:, at], axis=0, keepdims=True)

    if chunks * block > rows:
        acc[chunks - 1, pl.ds(rows - (chunks - 1) * block, chunks * block - rows), :] = jnp.zeros(
            (chunks * block - rows, dim), f32)
    per = TILES // chunks
    begun = []
    for i in range(TILES):
        student_tile(i)
        if (i + 1) % per == 0:
            stage(i // per, 0)
    for i in range(protos // LANES):
        proto_block(i)
    for k in range(1, nr):
        dw_copy(k).start()
        cd_copy(k).start()
    for t in range(1, 2 * nl + chunks):
        for g in range(chunks):
            if 1 <= t - g <= 2 * nl:
                stage(g, t - g)

    for k in range(1, nr):
        cd_copy(k).wait_recv()
        dw_copy(k).wait_recv()
    mine = pl.ds(pl.multiple_of(mx * share, 8), share)
    total = dw[mine, :]
    along = cd_out[...]
    for k in range(1, nr):
        total = total + dw_in[k - 1]
        along = along + cd_in[k - 1]
    gp[...] = (total - wn[mine, :] * along) * cs[...]

    for k in range(1, nr):
        cd_copy(k).wait_send()
        dw_copy(k).wait_send()
        for it in range(ITERS):
            col_copy(it, k).wait_send()
    for g in range(chunks):
        state[g] = (0, block)
        for l in range(nl):
            for k in range(1, orders[g][l][0]):
                red_copy(g, l, k).wait_send()
            state[g] = (0, state[g][1] // orders[g][l][0])
    for rd in range(ITERS + 2):
        pltpu.make_async_copy(rs_in.at[rd], rs_in.at[rd], rs_ss.at[rd]).wait()


def shards(n, nr, student, teacher, proto_raw, weights, mask):
    rows, dim = student.shape
    protos = proto_raw.shape[1]
    share = dim // nr
    levels = make_levels(n)
    nl = len(levels)
    chunks = TILES if rows % (TILES * n * 8) == 0 else 1
    piece = -(-rows // (chunks * n * 8)) * 8
    block = piece * n
    orders = [levels for g in range(chunks)]
    biggest = max(size for size, stride in levels)
    red_in = []
    for order in orders:
        ln = block
        for size, stride in order:
            ln //= size
            red_in.append(pltpu.VMEM((size - 1, ln, dim), f32))
    dma = pltpu.SemaphoreType.DMA
    rounds = ITERS + 2
    scratch = [
        pltpu.VMEM((dim, protos), f32),
        pltpu.VMEM((1, protos), f32),
        pltpu.VMEM((dim, protos), bf16),
        pltpu.VMEM((dim, protos), bf16),
        pltpu.VMEM((protos, 3 * dim), bf16),
        pltpu.VMEM((protos, rows), f32),
        pltpu.VMEM((protos, rows), f32),
        pltpu.VMEM((rows, dim), bf16),
        pltpu.VMEM((rows, dim), bf16),
        pltpu.VMEM((protos, rows), bf16),
        pltpu.VMEM((protos, rows), bf16),
        pltpu.VMEM((protos, LANES), f32),
        pltpu.VMEM((rounds, 1, rows), f32),
        pltpu.VMEM((rounds, n - 1, 1, rows), f32),
        pltpu.VMEM((ITERS, 1, protos), f32),
        pltpu.VMEM((ITERS, nr - 1, 1, protos), f32),
        pltpu.VMEM((chunks, block, dim), f32),
        pltpu.VMEM((dim, protos), f32),
        pltpu.VMEM((nr - 1, share, protos), f32),
        pltpu.VMEM((1, protos), f32),
        pltpu.VMEM((nr - 1, 1, protos), f32),
        dma((rounds,)), dma((rounds,)),
        dma((ITERS, nr - 1)), dma((ITERS, nr - 1)),
        dma((nr - 1,)), dma((nr - 1,)), dma((nr - 1,)), dma((nr - 1,)),
        dma((chunks, nl, biggest - 1)), dma((chunks, nl, biggest - 1)),
        dma((chunks, nl, biggest - 1)), dma((chunks, nl, biggest - 1)),
    ] + red_in
    vmem = pl.BlockSpec(memory_space=pltpu.VMEM)
    grad_student, grad_proto = pl.pallas_call(
        functools.partial(kernel, n, nr, chunks, block, orders),
        out_shape=(
            jax.ShapeDtypeStruct((chunks, block, dim), f32),
            jax.ShapeDtypeStruct((share, protos), f32),
        ),
        in_specs=[vmem] * 5,
        out_specs=(vmem, vmem),
        scratch_shapes=scratch,
        compiler_params=pltpu.CompilerParams(
            collective_id=0, has_side_effects=True, vmem_limit_bytes=56 * 1024 * 1024),
    )(student, teacher, proto_raw, weights.reshape(1, rows), mask.reshape(1, rows))
    return grad_student.reshape(chunks * block, dim)[:rows], grad_proto


def solution(mesh):
    n, nr = mesh.shape["proto"], mesh.shape["rows"]
    return jax.shard_map(
        functools.partial(shards, n, nr),
        mesh=mesh,
        in_specs=(P("rows", None), P("rows", None), P(None, "proto"), P("rows"), P("rows")),
        out_specs=(P("rows", None), P("rows", "proto")),
        check_vma=False,
    )
```

```python
import functools

import jax
import jax.numpy as jnp
from jax import lax
from jax.experimental import pallas as pl
from jax.experimental.pallas import tpu as pltpu
from jax.sharding import PartitionSpec as P

ITERS = 3
CHUNKS = 2
FILLS = (2, 1, 1, 1, 1, 1, 1)
EPS = 1e-06
TEACH = 1.0 / 0.07
STUDENT = 1.0 / 0.1
TILES = 4
LANES = 128
f32 = jnp.float32
bf16 = jnp.bfloat16
MESH = pl.DeviceIdType.MESH


def make_levels(n):
    if n % 2:
        return [(n, 1)]
    rest = n // 2
    outer = 4 if rest == 8 else 8
    while rest % outer:
        outer //= 2
    mid = rest // outer
    levels = [(2, 1), (mid, 2), (outer, 2 * mid)]
    return [lv for lv in levels if lv[0] > 1]


def split(x):
    hi = x.astype(bf16)
    return hi, (x - hi.astype(f32)).astype(bf16)


def dot(a, b):
    return jnp.dot(a, b, preferred_element_type=f32)


def dot_t(a, b):
    return lax.dot_general(a, b, (((1,), (1,)), ((), ())), preferred_element_type=f32)


def kernel(n, nr, chunks, block, orders, student, teacher, proto, weights, mask, gs, gp, *scratch):
    (wn, cs, w_hi, w_lo, lhs, kt, et, s_hi, s_lo, d_hi, d_lo, c128, rs_out, rs_in, cp_out, cp_in,
     acc, dw, dw_in, cd_out, cd_in, pe,
     rs_ss, rs_rs, cp_ss, cp_rs, dw_ss, dw_rs, cd_ss, cd_rs, red_ss, red_rs, gat_ss, gat_rs) = scratch[:34]
    red_in = scratch[34:]
    nl = len(orders[0])
    dim, protos = proto.shape
    rows = student.shape[0]
    tile = rows // TILES
    share = dim // nr
    me = lax.axis_index("proto")
    mx = lax.axis_index("rows")

    def peer(k):
        return {"proto": lax.rem(me + k, n)}

    def rpeer(k):
        return {"rows": lax.rem(mx + k, nr)}

    barrier = pltpu.get_barrier_semaphore()

    def greet(k, carry):
        pl.semaphore_signal(barrier, inc=1, device_id=peer(k), device_id_type=MESH)
        return carry

    lax.fori_loop(1, n, greet, 0)
    for k in range(1, nr):
        pl.semaphore_signal(barrier, inc=1, device_id=rpeer(k), device_id_type=MESH)

    for i in range(protos // LANES):
        cols = slice(i * LANES, (i + 1) * LANES)
        w = proto[:, cols]
        scale = lax.rsqrt(jnp.sum(w * w, axis=0, keepdims=True) + EPS)
        w = w * scale
        cs[:, cols] = scale
        wn[:, cols] = w
        hi, lo = split(w)
        w_hi[:, cols] = hi
        w_lo[:, cols] = lo
        hi, lo = split(w.T)
        lhs[cols, 0:dim] = hi
        lhs[cols, dim : 2 * dim] = hi
        lhs[cols, 2 * dim : 3 * dim] = lo

    def unit(x):
        return x * lax.rsqrt(jnp.sum(x * x, axis=1, keepdims=True) + EPS)

    def teach(i, carry):
        at = pl.ds(pl.multiple_of(i * tile, tile), tile)
        hi, lo = split(unit(teacher[at, :]))
        cos = dot_t(lhs[...], jnp.concatenate([hi, lo, hi], axis=1))
        q = jnp.exp(cos * TEACH)
        kt[:, at] = q
        rs_out[0, :, at] = jnp.sum(q, axis=0, keepdims=True)
        return carry

    def study(i, carry):
        at = pl.ds(pl.multiple_of(i * tile, tile), tile)
        hi, lo = split(unit(student[at, :]))
        s_hi[at, :] = hi
        s_lo[at, :] = lo
        cos = dot_t(lhs[...], jnp.concatenate([hi, lo, hi], axis=1))
        q = jnp.exp(cos * STUDENT)
        et[:, at] = q
        rs_out[ITERS + 1, :, at] = jnp.sum(q, axis=0, keepdims=True)
        return carry

    def row_start(rd):
        def send(k, carry):
            pltpu.make_async_remote_copy(
                rs_out.at[rd], rs_in.at[rd, k - 1], rs_ss.at[rd], rs_rs.at[rd],
                device_id=peer(k), device_id_type=MESH).start()
            return carry

        lax.fori_loop(1, n, send, 0)

    def row_total(rd):
        pltpu.make_async_copy(rs_in.at[rd], rs_in.at[rd], rs_rs.at[rd]).wait()
        return rs_out[rd] + jnp.sum(rs_in[rd], axis=0)

    def col_copy(it, k):
        return pltpu.make_async_remote_copy(
            cp_out.at[it], cp_in.at[it, k - 1], cp_ss.at[it, k - 1], cp_rs.at[it, k - 1],
            device_id=rpeer(k), device_id_type=MESH)

    lax.fori_loop(0, TILES, teach, 0)
    pl.semaphore_wait(barrier, n - 1 + nr - 1)
    row_start(0)
    def project(which, i, q):
        at = slice(i * tile, (i + 1) * tile)
        hi, lo = split(q)
        pe[which, :, at] = dot(w_hi[...], hi) + dot(w_lo[...], hi) + dot(w_hi[...], lo)

    def project_e(i):
        project(0, i, et[:, i * tile : (i + 1) * tile])

    def study_at(i):
        study(i, 0)

    todo = [functools.partial(study_at, i) for i in range(TILES)]
    todo.append(lambda: row_start(ITERS + 1))
    todo += [functools.partial(project_e, i) for i in range(TILES)]

    def fill(count):
        for step in range(min(count, len(todo))):
            todo.pop(0)()

    fill(FILLS[0])
    mask_f = mask[...].astype(f32)
    r = 1.0 / row_total(0)
    for it in range(ITERS):
        rm = r * mask_f
        for i in range(protos // LANES):
            at = slice(i * LANES, (i + 1) * LANES)
            part = kt[at, 0:LANES] * rm[:, 0:LANES]
            for j in range(1, rows // LANES):
                lane = slice(j * LANES, (j + 1) * LANES)
                part = part + kt[at, lane] * rm[:, lane]
            cp_out[it, :, at] = jnp.sum(part.T, axis=0, keepdims=True)
        for k in range(1, nr):
            col_copy(it, k).start()
        fill(FILLS[1 + 2 * it])
        total = cp_out[it]
        for k in range(1, nr):
            col_copy(it, k).wait_recv()
            total = total + cp_in[it, k - 1]
        c = 1.0 / total
        for i in range(protos // LANES):
            at = slice(i * LANES, (i + 1) * LANES)
            c128[at, :] = jnp.broadcast_to(c[:, at], (LANES, LANES)).T
        for j in range(rows // LANES):
            lane = slice(j * LANES, (j + 1) * LANES)
            rs_out[it + 1, :, lane] = jnp.sum(kt[:, lane] * c128[...], axis=0, keepdims=True)
        row_start(it + 1)
        fill(FILLS[2 + 2 * it])
        if it == ITERS - 1:
            fill(len(todo))
            for i in range(TILES):
                at = slice(i * tile, (i + 1) * tile)
                cc = jnp.concatenate([c128[...]] * (tile // LANES), axis=1)
                q = kt[:, at] * cc
                kt[:, at] = q
                project(1, i, q)
        r = 1.0 / row_total(it + 1)
    zsum = row_total(ITERS + 1)
    coef = weights[...] * mask_f * STUDENT
    pa = coef / zsum
    pb = coef * r

    state = [(0, block)] * chunks

    def place(g, l):
        size, stride = orders[g][l]
        return size, stride, lax.rem(me // stride, size)

    def red_copy(g, l, k):
        size, stride, mine = place(g, l)
        off, ln = state[g]
        sub = ln // size
        to = lax.rem(mine + k, size)
        return pltpu.make_async_remote_copy(
            acc.at[g, pl.ds(pl.multiple_of(off + to * sub, 8), sub)], red_in[g * nl + l].at[k - 1],
            red_ss.at[g, l, k - 1], red_rs.at[g, l, k - 1],
            device_id={"proto": me + (to - mine) * stride}, device_id_type=MESH)

    def red_start(g, l):
        for k in range(1, orders[g][l][0]):
            red_copy(g, l, k).start()

    def red_finish(g, l):
        size, stride, mine = place(g, l)
        off, ln = state[g]
        sub = ln // size
        for k in range(1, size):
            red_copy(g, l, k).wait_recv()
        off = pl.multiple_of(off + mine * sub, 8)
        at = pl.ds(off, sub)
        total = acc[g, at, :]
        for k in range(1, size):
            total = total + red_in[g * nl + l][k - 1]
        state[g] = (off, sub)
        if l < nl - 1:
            acc[g, at, :] = total
            return
        first = g * block + off
        first = pl.multiple_of(jnp.minimum(first, rows - sub), 8)
        st = student[pl.ds(first, sub), :]
        scale = lax.rsqrt(jnp.sum(st * st, axis=1, keepdims=True) + EPS)
        st = st * scale
        gs[g, at, :] = (total - st * jnp.sum(st * total, axis=1, keepdims=True)) * scale

    def gat_copy(g, l, k):
        size, stride, mine = place(g, l)
        off, ln = state[g]
        to = lax.rem(mine + k, size)
        at = pl.ds(pl.multiple_of(off, 8), ln)
        return pltpu.make_async_remote_copy(
            gs.at[g, at], gs.at[g, at], gat_ss.at[g, l, k - 1], gat_rs.at[g, l, k - 1],
            device_id={"proto": me + (to - mine) * stride}, device_id_type=MESH)

    def gat_start(g, l):
        for k in range(1, orders[g][l][0]):
            gat_copy(g, l, k).start()

    def gat_finish(g, l):
        size, stride, mine = place(g, l)
        off, ln = state[g]
        for k in range(1, size):
            gat_copy(g, l, k).wait_recv()
        for k in range(1, size):
            gat_copy(g, l, k).wait_send()
        state[g] = (off - mine * ln, ln * size)

    def stage(g, s):
        if s > 0:
            if s <= nl:
                red_finish(g, s - 1)
            else:
                gat_finish(g, 2 * nl - s)
        if s < nl:
            red_start(g, s)
        elif s < 2 * nl:
            gat_start(g, 2 * nl - 1 - s)

    def student_tile(i):
        at = slice(i * tile, (i + 1) * tile)
        part = (pe[0, :, at] * pa[:, at] - pe[1, :, at] * pb[:, at]).T
        for j in range(0, tile, min(tile, block)):
            g, first = divmod(i * tile + j, block)
            size = min(tile, block)
            acc[g, first : first + size, :] = part[j : j + size]

    def dcos_tile(i):
        at = slice(i * tile, (i + 1) * tile)
        hi, lo = split(et[:, at] * pa[:, at] - kt[:, at] * pb[:, at])
        d_hi[:, at] = hi
        d_lo[:, at] = lo

    def dw_copy(k):
        to = lax.rem(mx + k, nr)
        at = pl.ds(pl.multiple_of(to * share, 8), share)
        return pltpu.make_async_remote_copy(
            dw.at[at], dw_in.at[k - 1], dw_ss.at[k - 1], dw_rs.at[k - 1],
            device_id={"rows": to}, device_id_type=MESH)

    def cd_copy(k):
        return pltpu.make_async_remote_copy(
            cd_out, cd_in.at[k - 1], cd_ss.at[k - 1], cd_rs.at[k - 1],
            device_id=rpeer(k), device_id_type=MESH)

    def proto_block(i):
        at = slice(i * LANES, (i + 1) * LANES)
        hi = d_hi[at, :]
        part = (dot(hi, s_hi[...]) + dot(hi, s_lo[...]) + dot(d_lo[at, :], s_hi[...])).T
        dw[:, at] = part
        cd_out[:, at] = jnp.sum(part * wn[:, at], axis=0, keepdims=True)

    if chunks * block > rows:
        acc[chunks - 1, pl.ds(rows - (chunks - 1) * block, chunks * block - rows), :] = jnp.zeros(
            (chunks * block - rows, dim), f32)
    begun = 0
    for i in range(TILES):
        student_tile(i)
        while (begun + 1) * block <= (i + 1) * tile or (i == TILES - 1 and begun < chunks):
            stage(begun, 0)
            begun += 1
    for i in range(TILES):
        dcos_tile(i)
    for i in range(protos // LANES):
        proto_block(i)
    for k in range(1, nr):
        dw_copy(k).start()
        cd_copy(k).start()
    for t in range(1, 2 * nl + chunks):
        for g in range(chunks):
            if 1 <= t - g <= 2 * nl:
                stage(g, t - g)

    for k in range(1, nr):
        cd_copy(k).wait_recv()
        dw_copy(k).wait_recv()
    mine = pl.ds(pl.multiple_of(mx * share, 8), share)
    total = dw[mine, :]
    along = cd_out[...]
    for k in range(1, nr):
        total = total + dw_in[k - 1]
        along = along + cd_in[k - 1]
    gp[...] = (total - wn[mine, :] * along) * cs[...]

    for k in range(1, nr):
        cd_copy(k).wait_send()
        dw_copy(k).wait_send()
        for it in range(ITERS):
            col_copy(it, k).wait_send()
    for g in range(chunks):
        state[g] = (0, block)
        for l in range(nl):
            for k in range(1, orders[g][l][0]):
                red_copy(g, l, k).wait_send()
            state[g] = (0, state[g][1] // orders[g][l][0])
    for rd in range(ITERS + 2):
        pltpu.make_async_copy(rs_in.at[rd], rs_in.at[rd], rs_ss.at[rd]).wait()


def shards(n, nr, student, teacher, proto_raw, weights, mask):
    rows, dim = student.shape
    protos = proto_raw.shape[1]
    share = dim // nr
    levels = make_levels(n)
    nl = len(levels)
    chunks = CHUNKS if rows % (CHUNKS * n * 8) == 0 else 1
    piece = -(-rows // (chunks * n * 8)) * 8
    block = piece * n
    orders = [levels for g in range(chunks)]
    biggest = max(size for size, stride in levels)
    red_in = []
    for order in orders:
        ln = block
        for size, stride in order:
            ln //= size
            red_in.append(pltpu.VMEM((size - 1, ln, dim), f32))
    dma = pltpu.SemaphoreType.DMA
    rounds = ITERS + 2
    scratch = [
        pltpu.VMEM((dim, protos), f32),
        pltpu.VMEM((1, protos), f32),
        pltpu.VMEM((dim, protos), bf16),
        pltpu.VMEM((dim, protos), bf16),
        pltpu.VMEM((protos, 3 * dim), bf16),
        pltpu.VMEM((protos, rows), f32),
        pltpu.VMEM((protos, rows), f32),
        pltpu.VMEM((rows, dim), bf16),
        pltpu.VMEM((rows, dim), bf16),
        pltpu.VMEM((protos, rows), bf16),
        pltpu.VMEM((protos, rows), bf16),
        pltpu.VMEM((protos, LANES), f32),
        pltpu.VMEM((rounds, 1, rows), f32),
        pltpu.VMEM((rounds, n - 1, 1, rows), f32),
        pltpu.VMEM((ITERS, 1, protos), f32),
        pltpu.VMEM((ITERS, nr - 1, 1, protos), f32),
        pltpu.VMEM((chunks, block, dim), f32),
        pltpu.VMEM((dim, protos), f32),
        pltpu.VMEM((nr - 1, share, protos), f32),
        pltpu.VMEM((1, protos), f32),
        pltpu.VMEM((nr - 1, 1, protos), f32),
        pltpu.VMEM((2, dim, rows), f32),
        dma((rounds,)), dma((rounds,)),
        dma((ITERS, nr - 1)), dma((ITERS, nr - 1)),
        dma((nr - 1,)), dma((nr - 1,)), dma((nr - 1,)), dma((nr - 1,)),
        dma((chunks, nl, biggest - 1)), dma((chunks, nl, biggest - 1)),
        dma((chunks, nl, biggest - 1)), dma((chunks, nl, biggest - 1)),
    ] + red_in
    vmem = pl.BlockSpec(memory_space=pltpu.VMEM)
    grad_student, grad_proto = pl.pallas_call(
        functools.partial(kernel, n, nr, chunks, block, orders),
        out_shape=(
            jax.ShapeDtypeStruct((chunks, block, dim), f32),
            jax.ShapeDtypeStruct((share, protos), f32),
        ),
        in_specs=[vmem] * 5,
        out_specs=(vmem, vmem),
        scratch_shapes=scratch,
        compiler_params=pltpu.CompilerParams(
            collective_id=0, has_side_effects=True, vmem_limit_bytes=56 * 1024 * 1024),
    )(student, teacher, proto_raw, weights.reshape(1, rows), mask.reshape(1, rows))
    return grad_student.reshape(chunks * block, dim)[:rows], grad_proto


def solution(mesh):
    n, nr = mesh.shape["proto"], mesh.shape["rows"]
    return jax.shard_map(
        functools.partial(shards, n, nr),
        mesh=mesh,
        in_specs=(P("rows", None), P("rows", None), P(None, "proto"), P("rows"), P("rows")),
        out_specs=(P("rows", None), P("rows", "proto")),
        check_vma=False,
    )
```
